512 devices in a mesh: dp: 4 (over z_hi), tensor: 8 (over x, core), pre: 16 (over z_lo, y).
Axes of the slice: x: 4, y: 4, z: 16 (z_hi: 4, z_lo: 4; z = z_hi * 4 + z_lo), core: 2. Of those that a mesh axis runs over, the one named last changes fastest.
Arguments:
- grad_parts: bfloat16 [4, 32, 1024, 1024], P('dp', None, 'pre', 'tensor'), may hold values from -1.25 to 1.25
- slot_block: int32 [32], replicated, may hold values from 0 to 31, each once
- left_factor: float32 [32, 1024, 1024], P(('dp', 'tensor'), 'pre'), may hold values from -6 to 6
- right_factor: float32 [32, 1024, 1024], P(('dp', 'tensor'), 'pre'), may hold values from -6 to 6
- first_moment: float32 [32, 1024, 1024], P(('dp', 'tensor'), 'pre'), may hold values from -0.75 to 0.75
- second_moment: float32 [32, 1024, 1024], P(('dp', 'tensor'), 'pre'), may hold values from 0.001 to 0.01
- left_basis: bfloat16 [32, 1024, 1024], P(('dp', 'tensor'), 'pre'), may hold values from -0.1875 to 0.1875
- right_basis: bfloat16 [32, 1024, 1024], P(('dp', 'tensor'), 'pre'), may hold values from -0.1875 to 0.1875
- weight: bfloat16 [32, 1024, 1024], P(None, 'pre', 'tensor'), may hold values from -6 to 6
Outputs:
- new_left: float32 [32, 1024, 1024], P(('dp', 'tensor'), 'pre')
- new_right: float32 [32, 1024, 1024], P(('dp', 'tensor'), 'pre')
- new_first: float32 [32, 1024, 1024], P(('dp', 'tensor'), 'pre')
- new_second: float32 [32, 1024, 1024], P(('dp', 'tensor'), 'pre')
- update: bfloat16 [32, 1024, 1024], P(None, 'pre', 'tensor')
The draws below stay inside these ranges and needn't reach their ends.
Inputs may be any that keep to these rules, and one draw needn't show every extreme that they name: `slot_block`: each block is named by exactly one owner.
All inputs are finite; a program needn't handle non-finite values.
Results may differ from the reference program's by a relative error of at most 0.02.
Values may be sent and summed in bfloat16 or wider, within the bound.
A program may use at most 64 MiB of HBM per device.

```python
import math
import jax
import jax.numpy as jnp
from jax import lax

BLOCK = 1024
NBLK = 32
N_DP = 4


def block_levels(rng, dims, shards, smallest, top_value):
    level = 1.0
    for position, parts in shards:
        draws = jax.random.uniform(jax.random.fold_in(jax.random.fold_in(rng, 6), position), (parts,), jnp.float32, smallest / len(shards), top_value / len(shards))
        level = level * jnp.repeat(jnp.exp(draws), dims[position] // parts).reshape((-1,) + (1,) * (len(dims) - 1 - position))
    return level


def bell_draw(key, extent, scale, bound, shards=(), dtype=jnp.bfloat16):
    loudness = block_levels(key, extent, shards, -0.22, 0.18) if shards else 1.0
    entries = jax.random.normal(key, extent, jnp.float32) * scale * loudness
    return jnp.minimum(jnp.maximum(entries, -bound), bound).astype(dtype)


def setup_inputs(seed: int = 0) -> dict:
    splits = jax.random.split(jax.random.key(seed), 10)
    return {
        "grad_parts": bell_draw(splits[0], (N_DP, NBLK, BLOCK, BLOCK), (0.5 * BLOCK ** -0.25), 1.25, ((0, 4), (2, 16), (3, 8))),
        "slot_block": jax.random.permutation(splits[1], NBLK).astype(jnp.int32),
        "left_factor": bell_draw(splits[2], (NBLK, BLOCK, BLOCK), 1.0, 6.0, ((0, 32), (1, 16)), jnp.float32),
        "right_factor": bell_draw(splits[3], (NBLK, BLOCK, BLOCK), 1.0, 6.0, ((0, 32), (1, 16)), jnp.float32),
        "first_moment": bell_draw(splits[4], (NBLK, BLOCK, BLOCK), 0.05, 0.75, ((0, 32), (1, 16)), jnp.float32),
        "second_moment": jnp.clip(jnp.exp(math.log(0.01) - 2.30258502 * jax.random.uniform(splits[5], (NBLK, BLOCK, BLOCK), jnp.float32) ** block_levels(splits[5], (NBLK, BLOCK, BLOCK), ((0, 32), (1, 16)), -0.2, 0.2)), 0.001, 0.01),
        "left_basis": bell_draw(splits[6], (NBLK, BLOCK, BLOCK), BLOCK ** -0.5, 0.1875, ((0, 32), (1, 16))),
        "right_basis": bell_draw(splits[7], (NBLK, BLOCK, BLOCK), BLOCK ** -0.5, 0.1875, ((0, 32), (1, 16))),
        "weight": bell_draw(splits[8], (NBLK, BLOCK, BLOCK), 1.0, 6.0, ((1, 16), (2, 8))),
    }


factor_decay = 0.95
first_decay = 0.95
second_decay = 0.95
first_fix = 1.0 - (0.95 ** 10) ** 10
second_fix = 1.0 - (0.95 ** 10) ** 10
epsilon = 1e-08
weight_decay = 0.1

def reference(grad_parts, slot_block, left_factor, right_factor, first_moment, second_moment, left_basis, right_basis, weight):
    summed = lax.optimization_barrier(jnp.sum(grad_parts.astype(jnp.float32), axis=0)).astype(jnp.bfloat16)
    owned = jnp.take(summed, slot_block, axis=0)

    def single(items):
        gradient, left_old, right_old, first_old, second_old, basis_left, basis_right = items
        gram_left = jnp.dot(gradient, gradient.T, preferred_element_type=jnp.float32)
        gram_right = jnp.dot(gradient.T, gradient, preferred_element_type=jnp.float32)
        left_next = factor_decay * left_old + (1.0 - factor_decay) * gram_left
        right_next = factor_decay * right_old + (1.0 - factor_decay) * gram_right
        projected = jnp.dot(basis_left.T, gradient, preferred_element_type=jnp.float32).astype(jnp.bfloat16)
        rotated = jnp.dot(projected, basis_right, preferred_element_type=jnp.float32)
        first_next = first_decay * first_old + (1.0 - first_decay) * rotated
        second_next = second_decay * second_old + (1.0 - second_decay) * rotated * rotated
        direction = (first_next / first_fix / (jnp.sqrt(second_next / second_fix) + epsilon)).astype(jnp.bfloat16)
        counter = jnp.dot(direction, basis_right.T, preferred_element_type=jnp.float32).astype(jnp.bfloat16)
        unrotated = jnp.dot(basis_left, counter, preferred_element_type=jnp.float32).astype(jnp.bfloat16)
        return (left_next, right_next, first_next, second_next, unrotated)
    results = lax.map(single, (owned, left_factor, right_factor, first_moment, second_moment, left_basis, right_basis))
    placed = jnp.zeros_like(results[4]).at[slot_block].set(results[4])
    update = (placed.astype(jnp.float32) + weight_decay * weight.astype(jnp.float32)).astype(jnp.bfloat16)
    return (results[0], results[1], results[2], results[3], update)
```

```python
import jax
import jax.numpy as jnp
from jax import lax
from jax.experimental import pallas as pl
from jax.experimental.pallas import tpu as pltpu
from jax.sharding import PartitionSpec as P

factor_decay = 0.95
first_decay = 0.95
second_decay = 0.95
first_fix = 1.0 - (0.95**10) ** 10
second_fix = 1.0 - (0.95**10) ** 10
epsilon = 1e-08
weight_decay = 0.1

MESH = pl.DeviceIdType.MESH
F32 = jnp.float32
BF16 = jnp.bfloat16


def towards(zl, plane, parity):
    key = 2 * (zl - plane) + 2 * parity - 1
    return 2 * ((key + 16) // 16) - 1


def dot(a, b, dims=((1,), (0,))):
    return lax.dot_general(a, b, (dims, ((), ())), preferred_element_type=F32)


def kernel(
    slot, grad, left_old, right_old, first_old, second_old, basis_left, basis_right, weight,
    left_new, right_new, first_new, second_new, update,
    stage, rin, acc, gin, ghalf, qlh, qr, gfull, gturn, psend, precv, pfull, prow, rot, cbuf, cnt, unrot, land, inv,
    s1s, s1r, s2s, s2r, lzs, lzr, lys, lyr, rzs, rzr, rys, ryr, gzs, gzr, gys, gyr,
    pxs, pxr, prs, prr, cs, cr_, cxs, cxr, us, uf, ur,
):
    k, t, p = lax.axis_index("dp"), lax.axis_index("tensor"), lax.axis_index("pre")
    x, co, zl, y = t // 2, t % 2, p // 4, p % 4
    half = zl // 2
    tr = (zl % 2) * 4 + y
    up, down = (y + 1) % 4, (y + 3) % 4
    sent = []

    def push(src, dst, ssem, rsem, dev, here=None):
        copy = pltpu.make_async_remote_copy(
            src_ref=src, dst_ref=dst, send_sem=ssem, recv_sem=rsem, device_id=dev, device_id_type=MESH
        )
        if here is None:
            copy.start()
            sent.append((copy, None))
        else:
            away = jnp.logical_not(here)
            pl.when(away)(copy.start)
            pl.when(here)(pltpu.make_async_copy(src, dst, rsem).start)
            sent.append((copy, away))

    def arrived(dst, rsem):
        pltpu.make_async_copy(dst, dst, rsem).wait()

    for o in range(32):
        stage[(o // 8) * 8 + (o % 2) * 4 + (o % 8) // 2] = grad[slot[o]]
    signs = [towards(zl, 2 * c + t // 4, t % 2) for c in range(2)]
    for c in range(2):
        s = signs[c]
        d1, d2 = (k - s + 4) % 4, (k + 2) % 4
        push(stage.at[pl.ds(d1 * 8 + c * 4, 4)], rin.at[c, 0], s1s.at[c * 2], s1r.at[c * 2], (d1, t, p))
        push(
            stage.at[pl.ds(d2 * 8 + c * 4, 4)], rin.at[c, 1], s1s.at[c * 2 + 1], s1r.at[c * 2 + 1],
            ((k + s + 4) % 4, t, p),
        )

    for j in range(2):
        push(
            basis_left, qlh.at[pl.ds((p % 8) * 64, 64)], lzs.at[j], lzr.at[zl % 2],
            (k, x * 2 + half, (2 * co + j) * 4 + y),
            here=jnp.logical_and(half == co, zl % 2 == j),
        )
    own_rows = pl.ds(p * 64, 64)
    pltpu.make_async_copy(basis_right, qr.at[own_rows], rzr.at[zl]).start()
    for i in range(1, 4):
        push(basis_right, qr.at[own_rows], rzs.at[i - 1], rzr.at[zl], (k, t, ((zl + i) % 4) * 4 + y))

    slots = [slot[o] for o in range(32)]

    def invert(b, carry):
        total = jnp.int32(0)
        for o in range(32):
            place = (o // 8) * 8 + (o % 2) * 4 + (o % 8) // 2
            total = jnp.where(slots[o] == b, jnp.int32(place), total)
        inv[b] = total
        return carry

    lax.fori_loop(0, 32, invert, 0)

    def lrows(j, yy):
        return qlh.at[pl.ds((j * 4 + yy) * 64, 64)]

    for j in range(2):
        arrived(lrows(j, y), lzr.at[j])
        push(lrows(j, y), lrows(j, y), lys.at[j * 3], lyr.at[j * 3], (k, t, zl * 4 + up))
        push(lrows(j, y), lrows(j, y), lys.at[j * 3 + 1], lyr.at[j * 3 + 1], (k, t, zl * 4 + down))

    for c in range(2):
        s = signs[c]
        for way in range(2):
            arrived(rin.at[c, way], s1r.at[c * 2 + way])
            owner = k if way == 0 else (k + s + 4) % 4
            mine = stage[pl.ds(owner * 8 + c * 4, 4)]
            acc[c, way] = (mine.astype(F32) + rin[c, way].astype(F32)).astype(BF16)
            for xx in range(4):
                place = (owner, xx * 2 + half, (2 * c + t // 4) * 4 + t % 4)
                here = None
                if way == 0:
                    here = (xx * 2 + half == t) & (2 * c + t // 4 == zl) & (t % 4 == y)
                push(
                    acc.at[c, way, xx], gin.at[way, p % 8], s2s.at[c * 8 + way * 4 + xx], s2r.at[way * 8 + p % 8],
                    place, here,
                )

    arrived(lrows(0, down), lyr.at[0])
    push(lrows(0, down), lrows(0, down), lys.at[2], lyr.at[2], (k, t, zl * 4 + up))
    arrived(lrows(1, up), lyr.at[4])
    push(lrows(1, up), lrows(1, up), lys.at[5], lyr.at[5], (k, t, zl * 4 + down))

    def rrows(j, yy):
        return qr.at[pl.ds((j * 4 + yy) * 64, 64)]

    for j in range(4):
        arrived(rrows(j, y), rzr.at[j])
        push(rrows(j, y), rrows(j, y), rys.at[j * 3], ryr.at[j * 3], (k, t, zl * 4 + up))
        push(rrows(j, y), rrows(j, y), rys.at[j * 3 + 1], ryr.at[j * 3 + 1], (k, t, zl * 4 + down))

    for q in range(8):
        for way in range(2):
            arrived(gin.at[way, q], s2r.at[way * 8 + q])
        ghalf[pl.ds(q * 64, 64)] = (gin[0, q].astype(F32) + gin[1, q].astype(F32)).astype(BF16)

    arrived(lrows(1, down), lyr.at[3])
    arrived(lrows(0, up), lyr.at[1])
    opposite = (y + 2) % 4
    arrived(lrows(0, opposite), lyr.at[2])
    arrived(lrows(1, opposite), lyr.at[5])

    for n in range(2):
        lanes = pl.ds(pl.multiple_of((1 - co) * 512 + n * 256, 256), 256)
        psend[pl.ds(n * 256, 256)] = dot(qlh[:, lanes], ghalf[...], ((0,), (0,))).astype(BF16)
    push(psend, precv, pxs, pxr, (k, x * 2 + 1 - co, p))
    for j in range(4):
        push(
            ghalf, gfull.at[pl.ds(co * 512, 512), pl.ds(pl.multiple_of(tr * 128, 128), 128)],
            gzs.at[j], gzr.at[(zl % 2) * 2 + co], (k, x * 2 + half, j * 4 + y),
            here=(half == co) & (zl == j),
        )
    parts = []
    for n in range(2):
        lanes = pl.ds(pl.multiple_of(co * 512 + n * 256, 256), 256)
        parts.append(dot(qlh[:, lanes], ghalf[...], ((0,), (0,))))
    arrived(precv, pxr)
    for n in range(2):
        rows = pl.ds(n * 256, 256)
        pfull[rows] = (parts[n] + precv[rows].astype(F32)).astype(BF16)
    for q in range(8):
        push(
            pfull.at[pl.ds(q * 64, 64)], prow.at[:, pl.ds(pl.multiple_of(tr * 128, 128), 128)], prs.at[q], prr.at[tr],
            (k, x * 2 + half, co * 8 + q), here=(half == co) & (co * 8 + q == p),
        )

    for j in range(4):
        if j < 2:
            arrived(rrows(j, down), ryr.at[j * 3])
            push(rrows(j, down), rrows(j, down), rys.at[j * 3 + 2], ryr.at[j * 3 + 2], (k, t, zl * 4 + up))
        else:
            arrived(rrows(j, up), ryr.at[j * 3 + 1])
            push(rrows(j, up), rrows(j, up), rys.at[j * 3 + 2], ryr.at[j * 3 + 2], (k, t, zl * 4 + down))
    for j in range(4):
        if j < 2:
            arrived(rrows(j, up), ryr.at[j * 3 + 1])
        else:
            arrived(rrows(j, down), ryr.at[j * 3])
        arrived(rrows(j, opposite), ryr.at[j * 3 + 2])

    for tt in range(8):
        arrived(prow.at[:, pl.ds(tt * 128, 128)], prr.at[tt])
    for n in range(4):
        lanes = pl.ds(n * 256, 256)
        rotated = dot(prow[...], qr[:, lanes])
        first_next = first_decay * first_old[:, lanes] + (1.0 - first_decay) * rotated
        second_next = second_decay * second_old[:, lanes] + (1.0 - second_decay) * rotated * rotated
        first_new[:, lanes] = first_next
        second_new[:, lanes] = second_next
        rot[:, lanes] = (first_next / first_fix / (jnp.sqrt(second_next / second_fix) + epsilon)).astype(BF16)
    for n in range(4):
        cbuf[:, pl.ds(n * 256, 256)] = dot(rot[...], qr[pl.ds(n * 256, 256), :], ((1,), (1,))).astype(BF16)
        for tt in (2 * n, 2 * n + 1):
            push(
                cbuf.at[:, pl.ds(tt * 128, 128)], cnt.at[own_rows], cs.at[tt], cr_.at[p % 8],
                (k, x * 2 + half, (2 * co + tt // 4) * 4 + tt % 4), here=(half == co) & (tr == tt),
            )

    def gpart(tt, hh, yy):
        return gfull.at[pl.ds(hh * 512, 512), pl.ds(pl.multiple_of((tt * 4 + yy) * 128, 128), 128)]

    def gather_first(j):
        tt, hh = j // 2, j % 2
        arrived(gpart(tt, hh, y), gzr.at[j])
        push(gpart(tt, hh, y), gpart(tt, hh, y), gys.at[j * 3], gyr.at[j * 3], (k, t, zl * 4 + up))
        push(gpart(tt, hh, y), gpart(tt, hh, y), gys.at[j * 3 + 1], gyr.at[j * 3 + 1], (k, t, zl * 4 + down))

    def gather_relay(j):
        tt, hh = j // 2, j % 2
        if tt == 0:
            arrived(gpart(tt, hh, down), gyr.at[j * 3])
            push(gpart(tt, hh, down), gpart(tt, hh, down), gys.at[j * 3 + 2], gyr.at[j * 3 + 2], (k, t, zl * 4 + up))
        else:
            arrived(gpart(tt, hh, up), gyr.at[j * 3 + 1])
            push(gpart(tt, hh, up), gpart(tt, hh, up), gys.at[j * 3 + 2], gyr.at[j * 3 + 2], (k, t, zl * 4 + down))

    def gather_last(j):
        tt, hh = j // 2, j % 2
        if tt == 0:
            arrived(gpart(tt, hh, up), gyr.at[j * 3 + 1])
        else:
            arrived(gpart(tt, hh, down), gyr.at[j * 3])
        arrived(gpart(tt, hh, opposite), gyr.at[j * 3 + 2])

    for j in range(4):
        gather_first(j)

    def crows(hh, q):
        return cnt.at[pl.ds((hh * 8 + q) * 64, 64)]

    for q in range(8):
        arrived(crows(co, q), cr_.at[q])
        push(crows(co, q), crows(co, q), cxs.at[q], cxr.at[q], (k, x * 2 + 1 - co, p))
    for q in range(8):
        arrived(crows(1 - co, q), cxr.at[q])
    for n in range(2):
        unrot[pl.ds(n * 256, 256)] = dot(qlh[pl.ds(n * 256, 256), :], cnt[...]).astype(BF16)
        for q in range(n * 4, n * 4 + 4):
            s = towards(2 * co + q // 4, zl, tr % 2)
            index = k * 8 + half * 4 + x
            there = co * 8 + q
            push(
                unrot.at[pl.ds(q * 64, 64)], land.at[index], us.at[q * 2], ur.at[index], (k, tr, there),
                here=(tr == t) & (there == p),
            )
            push(
                unrot.at[pl.ds(q * 64, 64)], land.at[index], us.at[q * 2 + 1], ur.at[index],
                ((k - s + 4) % 4, tr, there),
            )

    for j in range(4):
        gather_relay(j)

    for c in range(2):
        s = signs[c]
        for xx in range(4):
            one, two = k * 8 + c * 4 + xx, ((k + s + 4) % 4) * 8 + c * 4 + xx
            arrived(land.at[one], ur.at[one])
            push(land.at[one], land.at[one], uf.at[c * 8 + xx], ur.at[one], ((k + s + 4) % 4, t, p))
            arrived(land.at[two], ur.at[two])
            push(land.at[two], land.at[two], uf.at[c * 8 + 4 + xx], ur.at[two], ((k - s + 4) % 4, t, p))

    for j in range(4):
        gather_last(j)
    gcols = gfull[:, pl.ds(pl.multiple_of((p // 2) * 128, 128), 128)]
    gturn[...] = gcols.astype(F32).T.astype(BF16)
    for n in range(4):
        lanes = pl.ds(n * 256, 256)
        left_new[:, lanes] = factor_decay * left_old[:, lanes] + (1.0 - factor_decay) * dot(
            gfull[own_rows, :], gfull[lanes, :], ((1,), (1,))
        )
    for n in range(4):
        lanes = pl.ds(n * 256, 256)
        right_new[:, lanes] = factor_decay * right_old[:, lanes] + (1.0 - factor_decay) * dot(
            gturn[pl.ds((p % 2) * 64, 64), :], gfull[:, lanes]
        )

    for c in range(2):
        s = signs[c]
        for xx in range(4):
            three, four = ((k - s + 4) % 4) * 8 + c * 4 + xx, ((k + 2) % 4) * 8 + c * 4 + xx
            arrived(land.at[three], ur.at[three])
            arrived(land.at[four], ur.at[four])

    for b in range(32):
        update[b] = (land[inv[b]].astype(F32) + weight_decay * weight[b].astype(F32)).astype(BF16)

    for copy, away in sent:
        if away is None:
            copy.wait_send()
        else:
            pl.when(away)(copy.wait_send)


def local(
    grad_parts, slot_block, left_factor, right_factor, first_moment, second_moment, left_basis, right_basis, weight
):
    vmem = pl.BlockSpec(memory_space=pltpu.VMEM)
    dma = lambda n: pltpu.SemaphoreType.DMA((n,))
    one = pltpu.SemaphoreType.DMA
    factor = jax.ShapeDtypeStruct((64, 1024), F32)
    outs = pl.pallas_call(
        kernel,
        out_shape=[factor] * 4 + [jax.ShapeDtypeStruct((32, 64, 128), BF16)],
        in_specs=[pl.BlockSpec(memory_space=pltpu.SMEM)] + [vmem] * 8,
        out_specs=[vmem] * 5,
        scratch_shapes=[
            pltpu.VMEM((32, 64, 128), BF16),
            pltpu.VMEM((2, 2, 4, 64, 128), BF16),
            pltpu.VMEM((2, 2, 4, 64, 128), BF16),
            pltpu.VMEM((2, 8, 64, 128), BF16),
            pltpu.VMEM((512, 128), BF16),
            pltpu.VMEM((512, 1024), BF16),
            pltpu.VMEM((1024, 1024), BF16),
            pltpu.VMEM((1024, 1024), BF16),
            pltpu.VMEM((128, 1024), BF16),
            pltpu.VMEM((512, 128), BF16),
            pltpu.VMEM((512, 128), BF16),
            pltpu.VMEM((512, 128), BF16),
            pltpu.VMEM((64, 1024), BF16),
            pltpu.VMEM((64, 1024), BF16),
            pltpu.VMEM((64, 1024), BF16),
            pltpu.VMEM((1024, 128), BF16),
            pltpu.VMEM((512, 128), BF16),
            pltpu.VMEM((32, 64, 128), BF16),
            pltpu.SMEM((32,), jnp.int32),
            dma(4), dma(4), dma(16), dma(16),
            dma(2), dma(2), dma(6), dma(6),
            dma(3), dma(4), dma(12), dma(12),
            dma(4), dma(4), dma(12), dma(12),
            one, one, dma(8), dma(8),
            dma(8), dma(8), dma(8), dma(8),
            dma(16), dma(16), dma(32),
        ],
        compiler_params=pltpu.CompilerParams(has_side_effects=True, vmem_limit_bytes=40 * 1024 * 1024),
        name="soap",
    )(
        slot_block, grad_parts[0], left_factor[0], right_factor[0], first_moment[0], second_moment[0],
        left_basis[0], right_basis[0], weight,
    )
    return outs[0][None], outs[1][None], outs[2][None], outs[3][None], outs[4]


def solution(mesh):
    owned = P(("dp", "tensor"), "pre", None)
    placed = P(None, "pre", "tensor")
    return jax.shard_map(
        local,
        mesh=mesh,
        in_specs=(P("dp", None, "pre", "tensor"), P(), owned, owned, owned, owned, owned, owned, placed),
        out_specs=(owned, owned, owned, owned, placed),
        check_vma=False,
    )
```

```python
import jax
import jax.numpy as jnp
from jax import lax
from jax.experimental import pallas as pl
from jax.experimental.pallas import tpu as pltpu
from jax.sharding import PartitionSpec as P

factor_decay = 0.95
first_decay = 0.95
second_decay = 0.95
first_fix = 1.0 - (0.95**10) ** 10
second_fix = 1.0 - (0.95**10) ** 10
epsilon = 1e-08
weight_decay = 0.1

MESH = pl.DeviceIdType.MESH
F32 = jnp.float32
BF16 = jnp.bfloat16


def towards(zl, plane, parity):
    key = 2 * (zl - plane) + 2 * parity - 1
    return 2 * ((key + 16) // 16) - 1


def dot(a, b, dims=((1,), (0,))):
    return lax.dot_general(a, b, (dims, ((), ())), preferred_element_type=F32)


def kernel(
    slot, grad_in, left_in, right_in, first_in, second_in, basis_left, basis_right, weight_in,
    left_out, right_out, first_out, second_out, update_out,
    grad, left_old, right_old, first_old, second_old, weight, left_new, right_new, first_new, second_new, update,
    ins, outs,
    stage, rin, acc, gin, ghalf, qlh, qr, gfull, gturn, pbuf, prow, rot, rotb, rotr, firstb, secondb, firstr, secondr, cbuf, cnt, unrot,
    land, inv, s1s, s1r, s2s, s2r, lts, ltr, lps, lpr, lys, lyr, rts, rtr, rps, rpr, rys, ryr, qxs, qxr, mts, mtr,
    xts, xtr, gramb, gramr, gts, gtr, gps, gpr, gys, gyr, gxs, gxr, prs, prr, cs, cr_, us, uf, ur,
):
    k, t, p = lax.axis_index("dp"), lax.axis_index("tensor"), lax.axis_index("pre")
    x, co, zl, y = t // 2, t % 2, p // 4, p % 4
    half = zl // 2
    tr = ((y - x + 4) % 4) * 2 + zl % 2
    seat = (zl % 2) * 4 + y
    up, down, opposite = (y + 1) % 4, (y + 3) % 4, (y + 2) % 4
    twin = (k, x * 2 + half, (2 * co + zl % 2) * 4 + y)
    row = (2 * co + zl % 2) * 4 + y
    pair = (k, t, (zl + 1 - 2 * (zl % 2)) * 4 + y)
    other = (k, x * 2 + 1 - co, p)
    sent = []

    def group(core, place):
        return (k, x * 2 + core, (2 * half + place // 4) * 4 + place % 4)

    def root(xx, c):
        return (xx * 2 + half, (2 * c + co) * 4 + (x + xx) % 4)

    def push(src, dst, ssem, rsem, dev, here=None):
        copy = pltpu.make_async_remote_copy(
            src_ref=src, dst_ref=dst, send_sem=ssem, recv_sem=rsem, device_id=dev, device_id_type=MESH
        )
        if here is None:
            copy.start()
            sent.append((copy, None))
        else:
            away = jnp.logical_not(here)
            pl.when(away)(copy.start)
            pl.when(here)(pltpu.make_async_copy(src, dst, rsem).start)
            sent.append((copy, away))

    def arrived(dst, rsem):
        pltpu.make_async_copy(dst, dst, rsem).wait()

    loads = [
        pltpu.make_async_copy(src, dst, ins.at[i])
        for i, (src, dst) in enumerate(
            [(grad_in, grad), (first_in, first_old), (second_in, second_old), (left_in, left_old),
             (right_in, right_old), (weight_in, weight)]
        )
    ]
    for load in loads:
        load.start()
    stores = [
        pltpu.make_async_copy(src, dst, outs.at[i])
        for i, (src, dst) in enumerate(
            [(first_new, first_out), (second_new, second_out), (left_new, left_out), (right_new, right_out),
             (update, update_out)]
        )
    ]

    barrier = pltpu.get_barrier_semaphore()
    met = 0

    def greet(dev, here=None):
        def call():
            pl.semaphore_signal(barrier, inc=1, device_id=dev, device_id_type=MESH)

        if here is None:
            call()
        else:
            pl.when(jnp.logical_not(here))(call)
        return 1 if here is None else jnp.where(here, 0, 1)

    signs = [towards(zl, 2 * c + co, co) for c in range(2)]
    for step in (1, 3):
        met += greet(((k + step) % 4, t, p))
    for tt in range(8):
        for hh in range(2):
            met += greet(group(hh, tt), (hh == co) & (tt == seat))
    met += greet(twin, half == co)
    for q in range(8):
        there = co * 8 + q
        s = towards(2 * co + q // 4, zl, tr % 2)
        met += greet((k, tr, there), (tr == t) & (there == p))
        met += greet(((k - s + 4) % 4, tr, there))
    for c in range(2):
        for xx in range(4):
            there = root(xx, c)
            met += greet((k, *there), (there[0] == t) & (there[1] == p))
            met += greet(((k + signs[c] + 4) % 4, *there))

    loads[0].wait()
    for o in range(32):
        stage[(o // 8) * 8 + (o % 2) * 4 + (o % 8) // 2] = grad[slot[o]]
    loads[1].wait()
    loads[2].wait()
    firstb[...] = first_old[...].astype(BF16)
    secondb[...] = second_old[...].astype(BF16)
    slots = [slot[o] for o in range(32)]

    def invert(b, carry):
        total = jnp.int32(0)
        for o in range(32):
            place = (o // 8) * 8 + (o % 2) * 4 + (o % 8) // 2
            total = jnp.where(slots[o] == b, jnp.int32(place), total)
        inv[b] = total
        return carry

    lax.fori_loop(0, 32, invert, 0)
    pl.semaphore_wait(barrier, met)
    for c in range(2):
        s = signs[c]
        d1, d2 = (k - s + 4) % 4, (k + 2) % 4
        push(stage.at[pl.ds(d1 * 8 + c * 4, 4)], rin.at[c, 0], s1s.at[c * 2], s1r.at[c * 2], (d1, t, p))
        push(
            stage.at[pl.ds(d2 * 8 + c * 4, 4)], rin.at[c, 1], s1s.at[c * 2 + 1], s1r.at[c * 2 + 1],
            ((k + s + 4) % 4, t, p),
        )

    def lrows(j, yy):
        return qlh.at[pl.ds((j * 4 + yy) * 64, 64)]

    def rrows(j, yy):
        return qr.at[pl.ds(((2 * co + j) * 4 + yy) * 64, 64)]

    own_rows = pl.ds(p * 64, 64)
    mine, pairs = zl % 2, 1 - zl % 2
    push(basis_left, qlh.at[pl.ds((p % 8) * 64, 64)], lts, ltr, twin, half == co)
    push(basis_right, qr.at[own_rows], rts, rtr, twin, half == co)

    def along_y(rows, j, slot_j, ss, rs):
        push(rows(j, y), rows(j, y), ss.at[slot_j * 3], rs.at[j * 3], (k, t, zl * 4 + up))
        push(rows(j, y), rows(j, y), ss.at[slot_j * 3 + 1], rs.at[j * 3 + 1], (k, t, zl * 4 + down))

    def from_pair(rows, pr_, ss, rs):
        arrived(rows(pairs, y), pr_)
        along_y(rows, pairs, 1, ss, rs)

    def from_twin(rows, tr_, ps, pr_, ss, rs):
        arrived(rows(mine, y), tr_)
        push(rows(mine, y), rows(mine, y), ps, pr_, pair)
        along_y(rows, mine, 0, ss, rs)

    def relay(rows, ss, rs):
        arrived(rows(0, down), rs.at[0])
        push(rows(0, down), rows(0, down), ss.at[6], rs.at[2], (k, t, zl * 4 + up))
        arrived(rows(1, up), rs.at[4])
        push(rows(1, up), rows(1, up), ss.at[7], rs.at[5], (k, t, zl * 4 + down))

    def rest(rows, rs):
        arrived(rows(1, down), rs.at[3])
        arrived(rows(0, up), rs.at[1])

    def last(rows, rs):
        arrived(rows(0, opposite), rs.at[2])
        arrived(rows(1, opposite), rs.at[5])

    def across(places):
        for j, yy, at in places:
            push(rrows(j, yy), rrows(j, yy), qxs.at[at], qxr.at[j * 4 + yy], other)

    from_twin(lrows, ltr, lps, lpr, lys, lyr)
    from_twin(rrows, rtr, rps, rpr, rys, ryr)
    from_pair(lrows, lpr, lys, lyr)
    from_pair(rrows, rpr, rys, ryr)

    for c in range(2):
        s = signs[c]
        for way in range(2):
            arrived(rin.at[c, way], s1r.at[c * 2 + way])
            owner = k if way == 0 else (k + s + 4) % 4
            own = stage[pl.ds(owner * 8 + c * 4, 4)]
            acc[c, way] = (own.astype(F32) + rin[c, way].astype(F32)).astype(BF16)
            for xx in range(4):
                place = (owner, *root(xx, c))
                here = None
                if way == 0:
                    here = (place[1] == t) & (place[2] == p)
                push(
                    acc.at[c, way, xx], gin.at[way, p % 8], s2s.at[c * 8 + way * 4 + xx], s2r.at[way * 8 + p % 8],
                    place, here,
                )

    push(firstb, firstr, mts.at[0], mtr.at[0], twin, half == co)
    push(secondb, secondr, mts.at[1], mtr.at[1], twin, half == co)
    relay(lrows, lys, lyr)
    relay(rrows, rys, ryr)
    across([(0, y, 0), (1, y, 1), (0, down, 2), (1, up, 3)])

    for q in range(8):
        for way in range(2):
            arrived(gin.at[way, q], s2r.at[way * 8 + q])
        ghalf[pl.ds(q * 64, 64)] = (gin[0, q].astype(F32) + gin[1, q].astype(F32)).astype(BF16)

    rest(lrows, lyr)
    last(lrows, lyr)

    gt = ghalf[...].astype(F32).T.astype(BF16)
    for n in range(4):
        turned = dot(gt, qlh[:, pl.ds(n * 256, 256)])
        pbuf[pl.ds(n * 256, 256)] = turned.T.astype(BF16)
        for there in range(n * 4, n * 4 + 4):
            push(
                pbuf.at[pl.ds(there * 64, 64)], prow.at[co, :, pl.ds(pl.multiple_of(tr * 128, 128), 128)],
                prs.at[there], prr.at[co * 8 + tr], group(there // 8, (there // 4) % 2 * 4 + there % 4), there == row,
            )
    def gpart(j, yy):
        column = ((yy - x + 4) % 4) * 2 + j
        return gfull.at[pl.ds(co * 512, 512), pl.ds(pl.multiple_of(column * 128, 128), 128)]

    def gacross(places):
        for j, yy, at in places:
            push(gpart(j, yy), gpart(j, yy), gxs.at[at], gxr.at[j * 4 + yy], other)

    gfull[pl.ds(co * 512, 512), pl.ds(pl.multiple_of(tr * 128, 128), 128)] = ghalf[...]
    push(gpart(mine, y), gpart(mine, y), gps, gpr, pair)
    along_y(gpart, mine, 0, gys, gyr)

    rest(rrows, ryr)
    across([(1, down, 4), (0, up, 5)])
    last(rrows, ryr)
    across([(0, opposite, 6), (1, opposite, 7)])
    for i in range(8):
        arrived(qr.at[pl.ds(((1 - co) * 8 + i) * 64, 64)], qxr.at[i])
    for i, ref in enumerate((firstr, secondr)):
        arrived(ref, mtr.at[i])

    for hh in range(2):
        for tt in range(8):
            arrived(prow.at[hh, :, pl.ds(tt * 128, 128)], prr.at[hh * 8 + tt])
    projected = (prow[0].astype(F32) + prow[1].astype(F32)).astype(BF16)
    for n in range(4):
        lanes = pl.ds(n * 256, 256)
        rotated = dot(projected, qr[:, lanes])
        rotb[:, lanes] = rotated.astype(BF16)
        first_next = first_decay * firstr[:, lanes].astype(F32) + (1.0 - first_decay) * rotated
        second_next = second_decay * secondr[:, lanes].astype(F32) + (1.0 - second_decay) * rotated * rotated
        rot[:, lanes] = (first_next / first_fix / (jnp.sqrt(second_next / second_fix) + epsilon)).astype(BF16)
    for n in range(4):
        cbuf[:, pl.ds(n * 256, 256)] = dot(rot[...], qr[pl.ds(n * 256, 256), :], ((1,), (1,))).astype(BF16)
        for tt in (2 * n, 2 * n + 1):
            for hh in range(2):
                push(
                    cbuf.at[:, pl.ds(tt * 128, 128)], cnt.at[pl.ds(row * 64, 64)], cs.at[hh * 8 + tt], cr_.at[row],
                    group(hh, tt % 2 * 4 + (tt // 2 + x) % 4), (hh == co) & (tr == tt),
                )
    push(rotb, rotr, xts, xtr, twin, half == co)

    from_pair(gpart, gpr, gys, gyr)
    gacross([(0, y, 0), (1, y, 1)])

    for q in range(16):
        arrived(cnt.at[pl.ds(q * 64, 64)], cr_.at[q])
    for n in range(2):
        unrot[pl.ds(n * 256, 256)] = dot(qlh[pl.ds(n * 256, 256), :], cnt[...]).astype(BF16)
        for q in range(n * 4, n * 4 + 4):
            s = towards(2 * co + q // 4, zl, tr % 2)
            index = k * 8 + half * 4 + x
            there = co * 8 + q
            push(
                unrot.at[pl.ds(q * 64, 64)], land.at[index], us.at[q * 2], ur.at[index], (k, tr, there),
                here=(tr == t) & (there == p),
            )
            push(
                unrot.at[pl.ds(q * 64, 64)], land.at[index], us.at[q * 2 + 1], ur.at[index],
                ((k - s + 4) % 4, tr, there),
            )

    relay(gpart, gys, gyr)
    gacross([(0, down, 2), (1, up, 3)])
    rest(gpart, gyr)
    gacross([(1, down, 4), (0, up, 5)])

    arrived(rotr, xtr)
    for n in range(4):
        lanes = pl.ds(n * 256, 256)
        rotated = rotr[:, lanes].astype(F32)
        first_new[:, lanes] = first_decay * first_old[:, lanes] + (1.0 - first_decay) * rotated
        second_new[:, lanes] = second_decay * second_old[:, lanes] + (1.0 - second_decay) * rotated * rotated
    stores[0].start()
    stores[1].start()

    for c in range(2):
        s = signs[c]
        for xx in range(4):
            one, two = k * 8 + c * 4 + xx, ((k + s + 4) % 4) * 8 + c * 4 + xx
            arrived(land.at[one], ur.at[one])
            push(land.at[one], land.at[one], uf.at[c * 8 + xx], ur.at[one], ((k + s + 4) % 4, t, p))
            arrived(land.at[two], ur.at[two])
            push(land.at[two], land.at[two], uf.at[c * 8 + 4 + xx], ur.at[two], ((k - s + 4) % 4, t, p))

    last(gpart, gyr)
    gacross([(0, opposite, 6), (1, opposite, 7)])
    for i in range(8):
        arrived(gfull.at[pl.ds((1 - co) * 512, 512), pl.ds(0, 128)], gxr.at[i])
    for n in range(4):
        lanes = pl.ds(n * 256, 256)
        gramb[0, :, lanes] = dot(gfull[pl.ds(row * 64, 64), :], gfull[lanes, :], ((1,), (1,))).astype(BF16)
    push(gramb.at[0], gramr.at[0], gts.at[0], gtr.at[0], twin, half == co)
    gcols = gfull[:, pl.ds(pl.multiple_of((row // 2) * 128, 128), 128)]
    gturn[...] = gcols.astype(F32).T.astype(BF16)
    for n in range(4):
        lanes = pl.ds(n * 256, 256)
        gramb[1, :, lanes] = dot(gturn[pl.ds((row % 2) * 64, 64), :], gfull[:, lanes]).astype(BF16)
    push(gramb.at[1], gramr.at[1], gts.at[1], gtr.at[1], twin, half == co)
    loads[3].wait()
    loads[4].wait()
    loads[5].wait()
    for i, (old, new) in enumerate(((left_old, left_new), (right_old, right_new))):
        arrived(gramr.at[i], gtr.at[i])
        new[...] = factor_decay * old[...] + (1.0 - factor_decay) * gramr[i].astype(F32)
        stores[2 + i].start()

    for c in range(2):
        s = signs[c]
        for xx in range(4):
            three, four = ((k - s + 4) % 4) * 8 + c * 4 + xx, ((k + 2) % 4) * 8 + c * 4 + xx
            arrived(land.at[three], ur.at[three])
            arrived(land.at[four], ur.at[four])

    for b in range(32):
        update[b] = (land[inv[b]].astype(F32) + weight_decay * weight[b].astype(F32)).astype(BF16)

    stores[4].start()
    for copy, away in sent:
        if away is None:
            copy.wait_send()
        else:
            pl.when(away)(copy.wait_send)
    for store in stores:
        store.wait()


def local(
    grad_parts, slot_block, left_factor, right_factor, first_moment, second_moment, left_basis, right_basis, weight
):
    anywhere = pl.BlockSpec(memory_space=pltpu.HBM)
    dma = lambda n: pltpu.SemaphoreType.DMA((n,))
    one = pltpu.SemaphoreType.DMA
    factor = jax.ShapeDtypeStruct((64, 1024), F32)
    outs = pl.pallas_call(
        kernel,
        out_shape=[factor] * 4 + [jax.ShapeDtypeStruct((32, 64, 128), BF16)],
        in_specs=[pl.BlockSpec(memory_space=pltpu.SMEM)] + [anywhere] * 8,
        out_specs=[anywhere] * 5,
        scratch_shapes=[
            pltpu.VMEM((32, 64, 128), BF16),
            *[pltpu.VMEM((64, 1024), F32)] * 4,
            pltpu.VMEM((32, 64, 128), BF16),
            *[pltpu.VMEM((64, 1024), F32)] * 4,
            pltpu.VMEM((32, 64, 128), BF16),
            dma(6), dma(5),
            pltpu.VMEM((32, 64, 128), BF16),
            pltpu.VMEM((2, 2, 4, 64, 128), BF16),
            pltpu.VMEM((2, 2, 4, 64, 128), BF16),
            pltpu.VMEM((2, 8, 64, 128), BF16),
            pltpu.VMEM((512, 128), BF16),
            pltpu.VMEM((512, 1024), BF16),
            pltpu.VMEM((1024, 1024), BF16),
            pltpu.VMEM((1024, 1024), BF16),
            pltpu.VMEM((128, 1024), BF16),
            pltpu.VMEM((1024, 128), BF16),
            pltpu.VMEM((2, 64, 1024), BF16),
            *[pltpu.VMEM((64, 1024), BF16)] * 8,
            pltpu.VMEM((1024, 128), BF16),
            pltpu.VMEM((512, 128), BF16),
            pltpu.VMEM((32, 64, 128), BF16),
            pltpu.SMEM((32,), jnp.int32),
            dma(4), dma(4), dma(16), dma(16),
            one, one, one, one, dma(8), dma(6),
            one, one, one, one, dma(8), dma(6),
            dma(8), dma(8), dma(2), dma(2), one, one,
            *[pltpu.VMEM((2, 64, 1024), BF16)] * 2,
            dma(2), dma(2), one, one, dma(8), dma(6), dma(8), dma(8),
            dma(16), dma(16), dma(16), dma(16),
            dma(16), dma(16), dma(32),
        ],
        compiler_params=pltpu.CompilerParams(collective_id=0, has_side_effects=True, vmem_limit_bytes=63 * 1024 * 1024),
        name="soap",
    )(
        slot_block, grad_parts[0], left_factor[0], right_factor[0], first_moment[0], second_moment[0],
        left_basis[0], right_basis[0], weight,
    )
    return outs[0][None], outs[1][None], outs[2][None], outs[3][None], outs[4]


def solution(mesh):
    owned = P(("dp", "tensor"), "pre", None)
    placed = P(None, "pre", "tensor")
    return jax.shard_map(
        local,
        mesh=mesh,
        in_specs=(P("dp", None, "pre", "tensor"), P(), owned, owned, owned, owned, owned, owned, placed),
        out_specs=(owned, owned, owned, owned, placed),
        check_vma=False,
    )
```

```python
import jax
import jax.numpy as jnp
from jax import lax
from jax.experimental import pallas as pl
from jax.experimental.pallas import tpu as pltpu
from jax.sharding import PartitionSpec as P

factor_decay = 0.95
first_decay = 0.95
second_decay = 0.95
first_fix = 1.0 - (0.95**10) ** 10
second_fix = 1.0 - (0.95**10) ** 10
epsilon = 1e-08
weight_decay = 0.1

MESH = pl.DeviceIdType.MESH
F32 = jnp.float32
BF16 = jnp.bfloat16


def towards(zl, plane, parity):
    key = 2 * (zl - plane) + 2 * parity - 1
    return 2 * ((key + 16) // 16) - 1


def dot(a, b, dims=((1,), (0,))):
    return lax.dot_general(a, b, (dims, ((), ())), preferred_element_type=F32)


def kernel(
    slot, grad_in, left_in, right_in, first_in, second_in, basis_left, basis_right, weight_in,
    left_out, right_out, first_out, second_out, update_out,
    grad, left_old, right_old, first_old, second_old, weight, left_new, right_new, first_new, second_new, update,
    ins, outs,
    stage, rin, acc, gin, ghalf, qlh, qr, gfull, gturn, pbuf, prow, rot, rotb, rotr, firstb, secondb, firstr, secondr, cbuf, cnt, unrot,
    land, inv, s1s, s1r, s2s, s2r, lts, ltr, lps, lpr, lys, lyr, rts, rtr, rps, rpr, rys, ryr, qxs, qxr, mts, mtr,
    xts, xtr, gramb, gramr, gts, gtr, gps, gpr, gys, gyr, gxs, gxr, prs, prr, cs, cr_, us, uf, ur,
):
    k, t, p = lax.axis_index("dp"), lax.axis_index("tensor"), lax.axis_index("pre")
    x, co, zl, y = t // 2, t % 2, p // 4, p % 4
    half = zl // 2
    tr = ((y - x + 4) % 4) * 2 + zl % 2
    seat = (zl % 2) * 4 + y
    up, down, opposite = (y + 1) % 4, (y + 3) % 4, (y + 2) % 4
    twin = (k, x * 2 + half, (2 * co + zl % 2) * 4 + y)
    row = (2 * co + zl % 2) * 4 + y
    pair = (k, t, (zl + 1 - 2 * (zl % 2)) * 4 + y)
    other = (k, x * 2 + 1 - co, p)
    sent = []

    def group(core, place):
        return (k, x * 2 + core, (2 * half + place // 4) * 4 + place % 4)

    def root(xx, c):
        return (xx * 2 + half, (2 * c + co) * 4 + (x + xx) % 4)

    def push(src, dst, ssem, rsem, dev, here=None):
        copy = pltpu.make_async_remote_copy(
            src_ref=src, dst_ref=dst, send_sem=ssem, recv_sem=rsem, device_id=dev, device_id_type=MESH
        )
        if here is None:
            copy.start()
            sent.append((copy, None))
        else:
            away = jnp.logical_not(here)
            pl.when(away)(copy.start)
            pl.when(here)(pltpu.make_async_copy(src, dst, rsem).start)
            sent.append((copy, away))

    def arrived(dst, rsem):
        pltpu.make_async_copy(dst, dst, rsem).wait()

    loads = [
        pltpu.make_async_copy(src, dst, ins.at[i])
        for i, (src, dst) in enumerate(
            [(grad_in, grad), (first_in, first_old), (second_in, second_old), (left_in, left_old),
             (right_in, right_old), (weight_in, weight)]
        )
    ]
    for load in loads:
        load.start()
    stores = [
        pltpu.make_async_copy(src, dst, outs.at[i])
        for i, (src, dst) in enumerate(
            [(first_new, first_out), (second_new, second_out), (left_new, left_out), (right_new, right_out),
             (update, update_out)]
        )
    ]

    barrier = pltpu.get_barrier_semaphore()
    met = 0

    def greet(dev, here=None):
        def call():
            pl.semaphore_signal(barrier, inc=1, device_id=dev, device_id_type=MESH)

        if here is None:
            call()
        else:
            pl.when(jnp.logical_not(here))(call)
        return 1 if here is None else jnp.where(here, 0, 1)

    signs = [towards(zl, 2 * c + co, co) for c in range(2)]
    for q in range(8):
        there = co * 8 + q
        s = towards(2 * co + q // 4, zl, tr % 2)
        met += greet((k, tr, there), (tr == t) & (there == p))
        met += greet(((k - s + 4) % 4, tr, there))
    for c in range(2):
        for xx in range(4):
            there = root(xx, c)
            met += greet((k, *there), (there[0] == t) & (there[1] == p))
            met += greet(((k + signs[c] + 4) % 4, *there))
    for step in (1, 3):
        met += greet(((k + step) % 4, t, p))
    for tt in range(8):
        for hh in range(2):
            met += greet(group(hh, tt), (hh == co) & (tt == seat))
    met += greet(twin, half == co)

    loads[0].wait()
    for o in range(32):
        stage[(o // 8) * 8 + (o % 2) * 4 + (o % 8) // 2] = grad[slot[o]]
    loads[1].wait()
    loads[2].wait()
    firstb[...] = first_old[...].astype(BF16)
    secondb[...] = second_old[...].astype(BF16)
    slots = [slot[o] for o in range(32)]

    def invert(b, carry):
        total = jnp.int32(0)
        for o in range(32):
            place = (o // 8) * 8 + (o % 2) * 4 + (o % 8) // 2
            total = jnp.where(slots[o] == b, jnp.int32(place), total)
        inv[b] = total
        return carry

    lax.fori_loop(0, 32, invert, 0)
    pl.semaphore_wait(barrier, met)
    own_rows = pl.ds(p * 64, 64)
    push(basis_left, qlh.at[pl.ds((p % 8) * 64, 64)], lts, ltr, twin, half == co)
    push(basis_right, qr.at[own_rows], rts, rtr, twin, half == co)
    for c in range(2):
        s = signs[c]
        for xx in range(4):
            for way, owner, there in ((0, (k - s + 4) % 4, (k - s + 4) % 4), (1, (k + 2) % 4, (k + s + 4) % 4)):
                at = c * 8 + way * 4 + xx
                push(stage.at[owner * 8 + c * 4 + xx], rin.at[c, way, xx], s1s.at[at], s1r.at[at], (there, t, p))

    def lrows(j, yy):
        return qlh.at[pl.ds((j * 4 + yy) * 64, 64)]

    def rrows(j, yy):
        return qr.at[pl.ds(((2 * co + j) * 4 + yy) * 64, 64)]

    own_rows = pl.ds(p * 64, 64)
    mine, pairs = zl % 2, 1 - zl % 2

    def along_y(rows, j, slot_j, ss, rs):
        push(rows(j, y), rows(j, y), ss.at[slot_j * 3], rs.at[j * 3], (k, t, zl * 4 + up))
        push(rows(j, y), rows(j, y), ss.at[slot_j * 3 + 1], rs.at[j * 3 + 1], (k, t, zl * 4 + down))

    def from_pair(rows, pr_, ss, rs):
        arrived(rows(pairs, y), pr_)
        along_y(rows, pairs, 1, ss, rs)

    def from_twin(rows, tr_, ps, pr_, ss, rs):
        arrived(rows(mine, y), tr_)
        push(rows(mine, y), rows(mine, y), ps, pr_, pair)
        along_y(rows, mine, 0, ss, rs)

    def relay(rows, ss, rs):
        arrived(rows(0, down), rs.at[0])
        push(rows(0, down), rows(0, down), ss.at[6], rs.at[2], (k, t, zl * 4 + up))
        arrived(rows(1, up), rs.at[4])
        push(rows(1, up), rows(1, up), ss.at[7], rs.at[5], (k, t, zl * 4 + down))

    def rest(rows, rs):
        arrived(rows(1, down), rs.at[3])
        arrived(rows(0, up), rs.at[1])

    def last(rows, rs):
        arrived(rows(0, opposite), rs.at[2])
        arrived(rows(1, opposite), rs.at[5])

    def across(places):
        for j, yy, at in places:
            push(rrows(j, yy), rrows(j, yy), qxs.at[at], qxr.at[j * 4 + yy], other)

    from_twin(lrows, ltr, lps, lpr, lys, lyr)
    from_twin(rrows, rtr, rps, rpr, rys, ryr)
    from_pair(lrows, lpr, lys, lyr)
    from_pair(rrows, rpr, rys, ryr)

    for c in range(2):
        s = signs[c]
        for xx in range(4):
            for way in range(2):
                at = c * 8 + way * 4 + xx
                arrived(rin.at[c, way, xx], s1r.at[at])
                owner = k if way == 0 else (k + s + 4) % 4
                own = stage[owner * 8 + c * 4 + xx]
                acc[c, way, xx] = (own.astype(F32) + rin[c, way, xx].astype(F32)).astype(BF16)
                place = (owner, *root(xx, c))
                here = (place[1] == t) & (place[2] == p) if way == 0 else None
                push(acc.at[c, way, xx], gin.at[way, p % 8], s2s.at[at], s2r.at[way * 8 + p % 8], place, here)

    push(firstb, firstr, mts.at[0], mtr.at[0], twin, half == co)
    push(secondb, secondr, mts.at[1], mtr.at[1], twin, half == co)
    relay(lrows, lys, lyr)
    relay(rrows, rys, ryr)
    across([(0, y, 0), (1, y, 1), (0, down, 2), (1, up, 3)])

    for q in range(8):
        for way in range(2):
            arrived(gin.at[way, q], s2r.at[way * 8 + q])
        ghalf[pl.ds(q * 64, 64)] = (gin[0, q].astype(F32) + gin[1, q].astype(F32)).astype(BF16)

    rest(lrows, lyr)
    last(lrows, lyr)

    gt = ghalf[...].astype(F32).T.astype(BF16)
    for n in range(4):
        turned = dot(gt, qlh[:, pl.ds(n * 256, 256)])
        pbuf[pl.ds(n * 256, 256)] = turned.T.astype(BF16)
        for there in range(n * 4, n * 4 + 4):
            push(
                pbuf.at[pl.ds(there * 64, 64)], prow.at[co, :, pl.ds(pl.multiple_of(tr * 128, 128), 128)],
                prs.at[there], prr.at[co * 8 + tr], group(there // 8, (there // 4) % 2 * 4 + there % 4), there == row,
            )
    def gpart(j, yy):
        column = ((yy - x + 4) % 4) * 2 + j
        return gfull.at[pl.ds(co * 512, 512), pl.ds(pl.multiple_of(column * 128, 128), 128)]

    def gacross(places):
        for j, yy, at in places:
            push(gpart(j, yy), gpart(j, yy), gxs.at[at], gxr.at[j * 4 + yy], other)

    gfull[pl.ds(co * 512, 512), pl.ds(pl.multiple_of(tr * 128, 128), 128)] = ghalf[...]
    push(gpart(mine, y), gpart(mine, y), gps, gpr, pair)
    along_y(gpart, mine, 0, gys, gyr)

    rest(rrows, ryr)
    across([(1, down, 4), (0, up, 5)])
    last(rrows, ryr)
    across([(0, opposite, 6), (1, opposite, 7)])
    for i in range(8):
        arrived(qr.at[pl.ds(((1 - co) * 8 + i) * 64, 64)], qxr.at[i])
    for i, ref in enumerate((firstr, secondr)):
        arrived(ref, mtr.at[i])

    for hh in range(2):
        for tt in range(8):
            arrived(prow.at[hh, :, pl.ds(tt * 128, 128)], prr.at[hh * 8 + tt])
    projected = (prow[0].astype(F32) + prow[1].astype(F32)).astype(BF16)
    for n in range(4):
        lanes = pl.ds(n * 256, 256)
        rotated = dot(projected, qr[:, lanes])
        rotb[:, lanes] = rotated.astype(BF16)
        first_next = first_decay * firstr[:, lanes].astype(F32) + (1.0 - first_decay) * rotated
        second_next = second_decay * secondr[:, lanes].astype(F32) + (1.0 - second_decay) * rotated * rotated
        rot[:, lanes] = (first_next / first_fix / (jnp.sqrt(second_next / second_fix) + epsilon)).astype(BF16)
    for n in range(4):
        cbuf[:, pl.ds(n * 256, 256)] = dot(rot[...], qr[pl.ds(n * 256, 256), :], ((1,), (1,))).astype(BF16)
        for tt in (2 * n, 2 * n + 1):
            for hh in range(2):
                push(
                    cbuf.at[:, pl.ds(tt * 128, 128)], cnt.at[pl.ds(row * 64, 64)], cs.at[hh * 8 + tt], cr_.at[row],
                    group(hh, tt % 2 * 4 + (tt // 2 + x) % 4), (hh == co) & (tr == tt),
                )
    push(rotb, rotr, xts, xtr, twin, half == co)

    from_pair(gpart, gpr, gys, gyr)
    gacross([(0, y, 0), (1, y, 1)])

    for q in range(16):
        arrived(cnt.at[pl.ds(q * 64, 64)], cr_.at[q])
    for n in range(2):
        unrot[pl.ds(n * 256, 256)] = dot(qlh[pl.ds(n * 256, 256), :], cnt[...]).astype(BF16)
        for q in range(n * 4, n * 4 + 4):
            s = towards(2 * co + q // 4, zl, tr % 2)
            index = k * 8 + half * 4 + x
            there = co * 8 + q
            push(
                unrot.at[pl.ds(q * 64, 64)], land.at[index], us.at[q * 2], ur.at[index], (k, tr, there),
                here=(tr == t) & (there == p),
            )
            push(
                unrot.at[pl.ds(q * 64, 64)], land.at[index], us.at[q * 2 + 1], ur.at[index],
                ((k - s + 4) % 4, tr, there),
            )

    relay(gpart, gys, gyr)
    gacross([(0, down, 2), (1, up, 3)])
    rest(gpart, gyr)
    gacross([(1, down, 4), (0, up, 5)])

    arrived(rotr, xtr)
    for n in range(4):
        lanes = pl.ds(n * 256, 256)
        rotated = rotr[:, lanes].astype(F32)
        first_new[:, lanes] = first_decay * first_old[:, lanes] + (1.0 - first_decay) * rotated
        second_new[:, lanes] = second_decay * second_old[:, lanes] + (1.0 - second_decay) * rotated * rotated
    stores[0].start()
    stores[1].start()

    for c in range(2):
        s = signs[c]
        for xx in range(4):
            one = k * 8 + c * 4 + xx
            arrived(land.at[one], ur.at[one])
            push(land.at[one], land.at[one], uf.at[c * 8 + xx], ur.at[one], ((k + s + 4) % 4, t, p))
    for c in range(2):
        s = signs[c]
        for xx in range(4):
            two = ((k + s + 4) % 4) * 8 + c * 4 + xx
            arrived(land.at[two], ur.at[two])
            push(land.at[two], land.at[two], uf.at[c * 8 + 4 + xx], ur.at[two], ((k - s + 4) % 4, t, p))

    last(gpart, gyr)
    gacross([(0, opposite, 6), (1, opposite, 7)])
    for i in range(8):
        arrived(gfull.at[pl.ds((1 - co) * 512, 512), pl.ds(0, 128)], gxr.at[i])
    for n in range(4):
        lanes = pl.ds(n * 256, 256)
        gramb[0, :, lanes] = dot(gfull[pl.ds(row * 64, 64), :], gfull[lanes, :], ((1,), (1,))).astype(BF16)
    push(gramb.at[0], gramr.at[0], gts.at[0], gtr.at[0], twin, half == co)
    gcols = gfull[:, pl.ds(pl.multiple_of((row // 2) * 128, 128), 128)]
    gturn[...] = gcols.astype(F32).T.astype(BF16)
    for n in range(4):
        lanes = pl.ds(n * 256, 256)
        gramb[1, :, lanes] = dot(gturn[pl.ds((row % 2) * 64, 64), :], gfull[:, lanes]).astype(BF16)
    push(gramb.at[1], gramr.at[1], gts.at[1], gtr.at[1], twin, half == co)
    loads[3].wait()
    loads[4].wait()
    loads[5].wait()
    for i, (old, new) in enumerate(((left_old, left_new), (right_old, right_new))):
        arrived(gramr.at[i], gtr.at[i])
        new[...] = factor_decay * old[...] + (1.0 - factor_decay) * gramr[i].astype(F32)
        stores[2 + i].start()

    for c in range(2):
        s = signs[c]
        for xx in range(4):
            three, four = ((k - s + 4) % 4) * 8 + c * 4 + xx, ((k + 2) % 4) * 8 + c * 4 + xx
            arrived(land.at[three], ur.at[three])
            arrived(land.at[four], ur.at[four])

    for b in range(32):
        update[b] = (land[inv[b]].astype(F32) + weight_decay * weight[b].astype(F32)).astype(BF16)

    stores[4].start()
    for copy, away in sent:
        if away is None:
            copy.wait_send()
        else:
            pl.when(away)(copy.wait_send)
    for store in stores:
        store.wait()


def hand_over(*refs):
    given, taken, held, ins, outs = refs[:5], refs[5:10], refs[10:15], refs[15], refs[16]
    reads = [pltpu.make_async_copy(given[i], held[i], ins.at[i]) for i in range(5)]
    writes = [pltpu.make_async_copy(held[i], taken[i], outs.at[i]) for i in range(5)]
    for read in reads:
        read.start()
    for read, write in zip(reads, writes):
        read.wait()
        write.start()
    for write in writes:
        write.wait()


def local(
    grad_parts, slot_block, left_factor, right_factor, first_moment, second_moment, left_basis, right_basis, weight
):
    anywhere = pl.BlockSpec(memory_space=pltpu.HBM)
    dma = lambda n: pltpu.SemaphoreType.DMA((n,))
    one = pltpu.SemaphoreType.DMA
    factor = jax.ShapeDtypeStruct((64, 1024), F32)
    outs = pl.pallas_call(
        kernel,
        out_shape=[factor] * 4 + [jax.ShapeDtypeStruct((32, 64, 128), BF16)],
        in_specs=[pl.BlockSpec(memory_space=pltpu.SMEM)] + [anywhere] * 8,
        out_specs=[anywhere] * 5,
        scratch_shapes=[
            pltpu.VMEM((32, 64, 128), BF16),
            *[pltpu.VMEM((64, 1024), F32)] * 4,
            pltpu.VMEM((32, 64, 128), BF16),
            *[pltpu.VMEM((64, 1024), F32)] * 4,
            pltpu.VMEM((32, 64, 128), BF16),
            dma(6), dma(5),
            pltpu.VMEM((32, 64, 128), BF16),
            pltpu.VMEM((2, 2, 4, 64, 128), BF16),
            pltpu.VMEM((2, 2, 4, 64, 128), BF16),
            pltpu.VMEM((2, 8, 64, 128), BF16),
            pltpu.VMEM((512, 128), BF16),
            pltpu.VMEM((512, 1024), BF16),
            pltpu.VMEM((1024, 1024), BF16),
            pltpu.VMEM((1024, 1024), BF16),
            pltpu.VMEM((128, 1024), BF16),
            pltpu.VMEM((1024, 128), BF16),
            pltpu.VMEM((2, 64, 1024), BF16),
            *[pltpu.VMEM((64, 1024), BF16)] * 8,
            pltpu.VMEM((1024, 128), BF16),
            pltpu.VMEM((512, 128), BF16),
            pltpu.VMEM((32, 64, 128), BF16),
            pltpu.SMEM((32,), jnp.int32),
            dma(16), dma(16), dma(16), dma(16),
            one, one, one, one, dma(8), dma(6),
            one, one, one, one, dma(8), dma(6),
            dma(8), dma(8), dma(2), dma(2), one, one,
            *[pltpu.VMEM((2, 64, 1024), BF16)] * 2,
            dma(2), dma(2), one, one, dma(8), dma(6), dma(8), dma(8),
            dma(16), dma(16), dma(16), dma(16),
            dma(16), dma(16), dma(32),
        ],
        compiler_params=pltpu.CompilerParams(collective_id=0, has_side_effects=True, vmem_limit_bytes=63 * 1024 * 1024),
        name="soap",
    )(
        slot_block, grad_parts[0], left_factor[0], right_factor[0], first_moment[0], second_moment[0],
        left_basis[0], right_basis[0], weight,
    )
    outs = pl.pallas_call(
        hand_over,
        out_shape=[factor] * 4 + [jax.ShapeDtypeStruct((32, 64, 128), BF16)],
        in_specs=[anywhere] * 5,
        out_specs=[anywhere] * 5,
        scratch_shapes=[*[pltpu.VMEM((64, 1024), F32)] * 4, pltpu.VMEM((32, 64, 128), BF16), dma(5), dma(5)],
        compiler_params=pltpu.CompilerParams(vmem_limit_bytes=63 * 1024 * 1024),
        name="hand_over",
    )(*outs)
    return outs[0][None], outs[1][None], outs[2][None], outs[3][None], outs[4]


def solution(mesh):
    owned = P(("dp", "tensor"), "pre", None)
    placed = P(None, "pre", "tensor")
    return jax.shard_map(
        local,
        mesh=mesh,
        in_specs=(P("dp", None, "pre", "tensor"), P(), owned, owned, owned, owned, owned, owned, placed),
        out_specs=(owned, owned, owned, owned, placed),
        check_vma=False,
    )
```

```python
import jax
import jax.numpy as jnp
from jax import lax
from jax.experimental import pallas as pl
from jax.experimental.pallas import tpu as pltpu
from jax.sharding import PartitionSpec as P

factor_decay = 0.95
first_decay = 0.95
second_decay = 0.95
first_fix = 1.0 - (0.95**10) ** 10
second_fix = 1.0 - (0.95**10) ** 10
epsilon = 1e-08
weight_decay = 0.1

MESH = pl.DeviceIdType.MESH
F32 = jnp.float32
BF16 = jnp.bfloat16


def towards(zl, plane, parity):
    key = 2 * (zl - plane) + 2 * parity - 1
    return 2 * ((key + 16) // 16) - 1


def dot(a, b, dims=((1,), (0,))):
    return lax.dot_general(a, b, (dims, ((), ())), preferred_element_type=F32)


def kernel(
    slot, grad_in, left_in, right_in, first_in, second_in, basis_left, basis_right, weight_in,
    left_out, right_out, first_out, second_out, update_out,
    grad, left_old, right_old, first_old, second_old, weight, left_new, right_new, first_new, second_new, update,
    ins, outs,
    stage, rin, acc, gin, ghalf, qlh, qr, gfull, gturn, pbuf, prow, rot, rotb, rotr, firstb, secondb, firstr, secondr, cbuf, cnt, unrot,
    land, inv, s1s, s1r, s2s, s2r, lts, ltr, lps, lpr, lys, lyr, rts, rtr, rps, rpr, rys, ryr, qxs, qxr, mts, mtr,
    xts, xtr, gramb, gramr, gts, gtr, gps, gpr, gys, gyr, gxs, gxr, prs, prr, cs, cr_, us, uf, ur,
):
    k, t, p = lax.axis_index("dp"), lax.axis_index("tensor"), lax.axis_index("pre")
    x, co, zl, y = t // 2, t % 2, p // 4, p % 4
    half = zl // 2
    tr = ((y - x + 4) % 4) * 2 + zl % 2
    seat = (zl % 2) * 4 + y
    up, down, opposite = (y + 1) % 4, (y + 3) % 4, (y + 2) % 4
    twin = (k, x * 2 + half, (2 * co + zl % 2) * 4 + y)
    row = (2 * co + zl % 2) * 4 + y
    pair = (k, t, (zl + 1 - 2 * (zl % 2)) * 4 + y)
    other = (k, x * 2 + 1 - co, p)
    sent = []

    def group(core, place):
        return (k, x * 2 + core, (2 * half + place // 4) * 4 + place % 4)

    def root(xx, c):
        return (xx * 2 + half, (2 * c + co) * 4 + (x + xx) % 4)

    def push(src, dst, ssem, rsem, dev, here=None):
        copy = pltpu.make_async_remote_copy(
            src_ref=src, dst_ref=dst, send_sem=ssem, recv_sem=rsem, device_id=dev, device_id_type=MESH
        )
        if here is None:
            copy.start()
            sent.append((copy, None))
        else:
            away = jnp.logical_not(here)
            pl.when(away)(copy.start)
            pl.when(here)(pltpu.make_async_copy(src, dst, rsem).start)
            sent.append((copy, away))

    def arrived(dst, rsem):
        pltpu.make_async_copy(dst, dst, rsem).wait()

    loads = [
        pltpu.make_async_copy(src, dst, ins.at[i])
        for i, (src, dst) in enumerate(
            [(grad_in, grad), (first_in, first_old), (second_in, second_old), (left_in, left_old),
             (right_in, right_old), (weight_in, weight)]
        )
    ]
    for load in loads:
        load.start()
    stores = [
        pltpu.make_async_copy(src, dst, outs.at[i])
        for i, (src, dst) in enumerate(
            [(first_new, first_out), (second_new, second_out), (left_new, left_out), (right_new, right_out),
             (update, update_out)]
        )
    ]

    barrier = pltpu.get_barrier_semaphore()
    met = 0

    def greet(dev, here=None):
        def call():
            pl.semaphore_signal(barrier, inc=1, device_id=dev, device_id_type=MESH)

        if here is None:
            call()
        else:
            pl.when(jnp.logical_not(here))(call)
        return 1 if here is None else jnp.where(here, 0, 1)

    signs = [towards(zl, 2 * c + co, co) for c in range(2)]
    for q in range(8):
        there = co * 8 + q
        s = towards(2 * co + q // 4, zl, tr % 2)
        met += greet((k, tr, there), (tr == t) & (there == p))
        met += greet(((k - s + 4) % 4, tr, there))
    for c in range(2):
        for xx in range(4):
            there = root(xx, c)
            met += greet((k, *there), (there[0] == t) & (there[1] == p))
            met += greet(((k + signs[c] + 4) % 4, *there))
    for step in (1, 3):
        met += greet(((k + step) % 4, t, p))
    for tt in range(8):
        for hh in range(2):
            met += greet(group(hh, tt), (hh == co) & (tt == seat))
    met += greet(twin, half == co)

    loads[0].wait()
    for o in range(32):
        stage[(o // 8) * 8 + (o % 2) * 4 + (o % 8) // 2] = grad[slot[o]]
    loads[1].wait()
    loads[2].wait()
    firstb[...] = first_old[...].astype(BF16)
    secondb[...] = second_old[...].astype(BF16)
    slots = [slot[o] for o in range(32)]

    def invert(b, carry):
        total = jnp.int32(0)
        for o in range(32):
            place = (o // 8) * 8 + (o % 2) * 4 + (o % 8) // 2
            total = jnp.where(slots[o] == b, jnp.int32(place), total)
        inv[b] = total
        return carry

    lax.fori_loop(0, 32, invert, 0)
    pl.semaphore_wait(barrier, met)
    own_rows = pl.ds(p * 64, 64)
    push(basis_left, qlh.at[pl.ds((p % 8) * 64, 64)], lts, ltr, twin, half == co)
    push(basis_right, qr.at[own_rows], rts, rtr, twin, half == co)
    for c in range(2):
        s = signs[c]
        for xx in range(4):
            for way, owner, there in ((0, (k - s + 4) % 4, (k - s + 4) % 4), (1, (k + 2) % 4, (k + s + 4) % 4)):
                at = c * 8 + way * 4 + xx
                push(stage.at[owner * 8 + c * 4 + xx], rin.at[c, way, xx], s1s.at[at], s1r.at[at], (there, t, p))

    def lrows(j, yy):
        return qlh.at[pl.ds((j * 4 + yy) * 64, 64)]

    def rrows(j, yy):
        return qr.at[pl.ds(((2 * co + j) * 4 + yy) * 64, 64)]

    own_rows = pl.ds(p * 64, 64)
    mine, pairs = zl % 2, 1 - zl % 2

    def along_y(rows, j, slot_j, ss, rs):
        push(rows(j, y), rows(j, y), ss.at[slot_j * 3], rs.at[j * 3], (k, t, zl * 4 + up))
        push(rows(j, y), rows(j, y), ss.at[slot_j * 3 + 1], rs.at[j * 3 + 1], (k, t, zl * 4 + down))

    def from_pair(rows, pr_, ss, rs):
        arrived(rows(pairs, y), pr_)
        along_y(rows, pairs, 1, ss, rs)

    def from_twin(rows, tr_, ps, pr_, ss, rs):
        arrived(rows(mine, y), tr_)
        push(rows(mine, y), rows(mine, y), ps, pr_, pair)
        along_y(rows, mine, 0, ss, rs)

    def relay(rows, ss, rs):
        arrived(rows(0, down), rs.at[0])
        push(rows(0, down), rows(0, down), ss.at[6], rs.at[2], (k, t, zl * 4 + up))
        arrived(rows(1, up), rs.at[4])
        push(rows(1, up), rows(1, up), ss.at[7], rs.at[5], (k, t, zl * 4 + down))

    def rest(rows, rs):
        arrived(rows(1, down), rs.at[3])
        arrived(rows(0, up), rs.at[1])

    def last(rows, rs):
        arrived(rows(0, opposite), rs.at[2])
        arrived(rows(1, opposite), rs.at[5])

    def across(places):
        for j, yy, at in places:
            push(rrows(j, yy), rrows(j, yy), qxs.at[at], qxr.at[j * 4 + yy], other)

    from_twin(lrows, ltr, lps, lpr, lys, lyr)
    from_twin(rrows, rtr, rps, rpr, rys, ryr)
    from_pair(lrows, lpr, lys, lyr)
    from_pair(rrows, rpr, rys, ryr)

    for c in range(2):
        s = signs[c]
        for xx in range(4):
            for way in range(2):
                at = c * 8 + way * 4 + xx
                arrived(rin.at[c, way, xx], s1r.at[at])
                owner = k if way == 0 else (k + s + 4) % 4
                own = stage[owner * 8 + c * 4 + xx]
                acc[c, way, xx] = (own.astype(F32) + rin[c, way, xx].astype(F32)).astype(BF16)
                place = (owner, *root(xx, c))
                here = (place[1] == t) & (place[2] == p) if way == 0 else None
                push(acc.at[c, way, xx], gin.at[way, p % 8], s2s.at[at], s2r.at[way * 8 + p % 8], place, here)

    push(firstb, firstr, mts.at[0], mtr.at[0], twin, half == co)
    push(secondb, secondr, mts.at[1], mtr.at[1], twin, half == co)
    relay(lrows, lys, lyr)
    relay(rrows, rys, ryr)
    across([(0, y, 0), (1, y, 1), (0, down, 2), (1, up, 3)])

    for q in range(8):
        for way in range(2):
            arrived(gin.at[way, q], s2r.at[way * 8 + q])
        ghalf[pl.ds(q * 64, 64)] = (gin[0, q].astype(F32) + gin[1, q].astype(F32)).astype(BF16)

    rest(lrows, lyr)
    last(lrows, lyr)

    gt = ghalf[...].astype(F32).T.astype(BF16)
    for n in range(4):
        turned = dot(gt, qlh[:, pl.ds(n * 256, 256)])
        pbuf[pl.ds(n * 256, 256)] = turned.T.astype(BF16)
        for there in range(n * 4, n * 4 + 4):
            push(
                pbuf.at[pl.ds(there * 64, 64)], prow.at[co, :, pl.ds(pl.multiple_of(tr * 128, 128), 128)],
                prs.at[there], prr.at[co * 8 + tr], group(there // 8, (there // 4) % 2 * 4 + there % 4), there == row,
            )
    def gpart(j, yy):
        column = ((yy - x + 4) % 4) * 2 + j
        return gfull.at[pl.ds(co * 512, 512), pl.ds(pl.multiple_of(column * 128, 128), 128)]

    def gacross(places):
        for j, yy, at in places:
            push(gpart(j, yy), gpart(j, yy), gxs.at[at], gxr.at[j * 4 + yy], other)

    gfull[pl.ds(co * 512, 512), pl.ds(pl.multiple_of(tr * 128, 128), 128)] = ghalf[...]
    push(gpart(mine, y), gpart(mine, y), gps, gpr, pair)
    along_y(gpart, mine, 0, gys, gyr)

    rest(rrows, ryr)
    across([(1, down, 4), (0, up, 5)])
    last(rrows, ryr)
    across([(0, opposite, 6), (1, opposite, 7)])
    for i in range(8):
        arrived(qr.at[pl.ds(((1 - co) * 8 + i) * 64, 64)], qxr.at[i])
    for i, ref in enumerate((firstr, secondr)):
        arrived(ref, mtr.at[i])

    for hh in range(2):
        for tt in range(8):
            arrived(prow.at[hh, :, pl.ds(tt * 128, 128)], prr.at[hh * 8 + tt])
    projected = (prow[0].astype(F32) + prow[1].astype(F32)).astype(BF16)
    for n in range(4):
        lanes = pl.ds(n * 256, 256)
        rotated = dot(projected, qr[:, lanes])
        rotb[:, lanes] = rotated.astype(BF16)
        first_next = first_decay * firstr[:, lanes].astype(F32) + (1.0 - first_decay) * rotated
        second_next = second_decay * secondr[:, lanes].astype(F32) + (1.0 - second_decay) * rotated * rotated
        rot[:, lanes] = (first_next / first_fix / (jnp.sqrt(second_next / second_fix) + epsilon)).astype(BF16)
    for n in range(4):
        cbuf[:, pl.ds(n * 256, 256)] = dot(rot[...], qr[pl.ds(n * 256, 256), :], ((1,), (1,))).astype(BF16)
        for tt in (2 * n, 2 * n + 1):
            for hh in range(2):
                push(
                    cbuf.at[:, pl.ds(tt * 128, 128)], cnt.at[pl.ds(row * 64, 64)], cs.at[hh * 8 + tt], cr_.at[row],
                    group(hh, tt % 2 * 4 + (tt // 2 + x) % 4), (hh == co) & (tr == tt),
                )
    push(rotb, rotr, xts, xtr, twin, half == co)

    from_pair(gpart, gpr, gys, gyr)
    gacross([(0, y, 0), (1, y, 1)])

    for q in range(16):
        arrived(cnt.at[pl.ds(q * 64, 64)], cr_.at[q])
    for n in range(2):
        unrot[pl.ds(n * 256, 256)] = dot(qlh[pl.ds(n * 256, 256), :], cnt[...]).astype(BF16)
        for q in range(n * 4, n * 4 + 4):
            s = towards(2 * co + q // 4, zl, tr % 2)
            index = k * 8 + half * 4 + x
            there = co * 8 + q
            push(
                unrot.at[pl.ds(q * 64, 64)], land.at[index], us.at[q * 2 + 1], ur.at[index],
                ((k - s + 4) % 4, tr, there),
            )
            push(
                unrot.at[pl.ds(q * 64, 64)], land.at[index], us.at[q * 2], ur.at[index], (k, tr, there),
                here=(tr == t) & (there == p),
            )

    relay(gpart, gys, gyr)
    gacross([(0, down, 2), (1, up, 3)])

    for c in range(2):
        s = signs[c]
        for xx in range(4):
            one = k * 8 + c * 4 + xx
            arrived(land.at[one], ur.at[one])
            push(land.at[one], land.at[one], uf.at[c * 8 + xx], ur.at[one], ((k + s + 4) % 4, t, p))
    for c in range(2):
        s = signs[c]
        for xx in range(4):
            two = ((k + s + 4) % 4) * 8 + c * 4 + xx
            arrived(land.at[two], ur.at[two])
            push(land.at[two], land.at[two], uf.at[c * 8 + 4 + xx], ur.at[two], ((k - s + 4) % 4, t, p))

    rest(gpart, gyr)
    gacross([(1, down, 4), (0, up, 5)])

    arrived(rotr, xtr)
    for n in range(4):
        lanes = pl.ds(n * 256, 256)
        rotated = rotr[:, lanes].astype(F32)
        first_new[:, lanes] = first_decay * first_old[:, lanes] + (1.0 - first_decay) * rotated
        second_new[:, lanes] = second_decay * second_old[:, lanes] + (1.0 - second_decay) * rotated * rotated
    stores[0].start()
    stores[1].start()

    last(gpart, gyr)
    gacross([(0, opposite, 6), (1, opposite, 7)])
    for i in range(8):
        arrived(gfull.at[pl.ds((1 - co) * 512, 512), pl.ds(0, 128)], gxr.at[i])
    for n in range(4):
        lanes = pl.ds(n * 256, 256)
        gramb[0, :, lanes] = dot(gfull[pl.ds(row * 64, 64), :], gfull[lanes, :], ((1,), (1,))).astype(BF16)
    push(gramb.at[0], gramr.at[0], gts.at[0], gtr.at[0], twin, half == co)
    gcols = gfull[:, pl.ds(pl.multiple_of((row // 2) * 128, 128), 128)]
    gturn[...] = gcols.astype(F32).T.astype(BF16)
    for n in range(4):
        lanes = pl.ds(n * 256, 256)
        gramb[1, :, lanes] = dot(gturn[pl.ds((row % 2) * 64, 64), :], gfull[:, lanes]).astype(BF16)
    push(gramb.at[1], gramr.at[1], gts.at[1], gtr.at[1], twin, half == co)
    loads[3].wait()
    loads[4].wait()
    loads[5].wait()
    for i, (old, new) in enumerate(((left_old, left_new), (right_old, right_new))):
        arrived(gramr.at[i], gtr.at[i])
        new[...] = factor_decay * old[...] + (1.0 - factor_decay) * gramr[i].astype(F32)
        stores[2 + i].start()

    for c in range(2):
        s = signs[c]
        for xx in range(4):
            three, four = ((k - s + 4) % 4) * 8 + c * 4 + xx, ((k + 2) % 4) * 8 + c * 4 + xx
            arrived(land.at[three], ur.at[three])
            arrived(land.at[four], ur.at[four])

    for b in range(32):
        update[b] = (land[inv[b]].astype(F32) + weight_decay * weight[b].astype(F32)).astype(BF16)

    stores[4].start()
    for copy, away in sent:
        if away is None:
            copy.wait_send()
        else:
            pl.when(away)(copy.wait_send)
    for store in stores:
        store.wait()


def hand_over(*refs):
    given, taken, held, ins, outs = refs[:5], refs[5:10], refs[10:15], refs[15], refs[16]
    reads = [pltpu.make_async_copy(given[i], held[i], ins.at[i]) for i in range(5)]
    writes = [pltpu.make_async_copy(held[i], taken[i], outs.at[i]) for i in range(5)]
    for read in reads:
        read.start()
    for read, write in zip(reads, writes):
        read.wait()
        write.start()
    for write in writes:
        write.wait()


def local(
    grad_parts, slot_block, left_factor, right_factor, first_moment, second_moment, left_basis, right_basis, weight
):
    anywhere = pl.BlockSpec(memory_space=pltpu.HBM)
    dma = lambda n: pltpu.SemaphoreType.DMA((n,))
    one = pltpu.SemaphoreType.DMA
    factor = jax.ShapeDtypeStruct((64, 1024), F32)
    outs = pl.pallas_call(
        kernel,
        out_shape=[factor] * 4 + [jax.ShapeDtypeStruct((32, 64, 128), BF16)],
        in_specs=[pl.BlockSpec(memory_space=pltpu.SMEM)] + [anywhere] * 8,
        out_specs=[anywhere] * 5,
        scratch_shapes=[
            pltpu.VMEM((32, 64, 128), BF16),
            *[pltpu.VMEM((64, 1024), F32)] * 4,
            pltpu.VMEM((32, 64, 128), BF16),
            *[pltpu.VMEM((64, 1024), F32)] * 4,
            pltpu.VMEM((32, 64, 128), BF16),
            dma(6), dma(5),
            pltpu.VMEM((32, 64, 128), BF16),
            pltpu.VMEM((2, 2, 4, 64, 128), BF16),
            pltpu.VMEM((2, 2, 4, 64, 128), BF16),
            pltpu.VMEM((2, 8, 64, 128), BF16),
            pltpu.VMEM((512, 128), BF16),
            pltpu.VMEM((512, 1024), BF16),
            pltpu.VMEM((1024, 1024), BF16),
            pltpu.VMEM((1024, 1024), BF16),
            pltpu.VMEM((128, 1024), BF16),
            pltpu.VMEM((1024, 128), BF16),
            pltpu.VMEM((2, 64, 1024), BF16),
            *[pltpu.VMEM((64, 1024), BF16)] * 8,
            pltpu.VMEM((1024, 128), BF16),
            pltpu.VMEM((512, 128), BF16),
            pltpu.VMEM((32, 64, 128), BF16),
            pltpu.SMEM((32,), jnp.int32),
            dma(16), dma(16), dma(16), dma(16),
            one, one, one, one, dma(8), dma(6),
            one, one, one, one, dma(8), dma(6),
            dma(8), dma(8), dma(2), dma(2), one, one,
            *[pltpu.VMEM((2, 64, 1024), BF16)] * 2,
            dma(2), dma(2), one, one, dma(8), dma(6), dma(8), dma(8),
            dma(16), dma(16), dma(16), dma(16),
            dma(16), dma(16), dma(32),
        ],
        compiler_params=pltpu.CompilerParams(collective_id=0, has_side_effects=True, vmem_limit_bytes=63 * 1024 * 1024),
        name="soap",
    )(
        slot_block, grad_parts[0], left_factor[0], right_factor[0], first_moment[0], second_moment[0],
        left_basis[0], right_basis[0], weight,
    )
    outs = pl.pallas_call(
        hand_over,
        out_shape=[factor] * 4 + [jax.ShapeDtypeStruct((32, 64, 128), BF16)],
        in_specs=[anywhere] * 5,
        out_specs=[anywhere] * 5,
        scratch_shapes=[*[pltpu.VMEM((64, 1024), F32)] * 4, pltpu.VMEM((32, 64, 128), BF16), dma(5), dma(5)],
        compiler_params=pltpu.CompilerParams(vmem_limit_bytes=63 * 1024 * 1024),
        name="hand_over",
    )(*outs)
    return outs[0][None], outs[1][None], outs[2][None], outs[3][None], outs[4]


def solution(mesh):
    owned = P(("dp", "tensor"), "pre", None)
    placed = P(None, "pre", "tensor")
    return jax.shard_map(
        local,
        mesh=mesh,
        in_specs=(P("dp", None, "pre", "tensor"), P(), owned, owned, owned, owned, owned, owned, placed),
        out_specs=(owned, owned, owned, owned, placed),
        check_vma=False,
    )
```
